512 devices in a mesh: pair: 16 (over z), virt: 32 (over y, x, core).
Axes of the slice: x: 4, y: 4, z: 16, core: 2. Of those that a mesh axis runs over, the one named last changes fastest.
Arguments:
- amplitudes: bfloat16 [14336, 65536], P('pair', 'virt'), may hold values from -6 to 6
- mask_amp: int32 [112, 512], P('pair', 'virt'), may hold values from 0 to 1, as said below
- integrals: bfloat16 [65536, 1024], P('virt', 'pair'), may hold values from -0.09375 to 0.09375
- mask_int: int32 [512, 8], P('virt'), may hold values 0 or 1
Outputs:
- ladder: bfloat16 [14336, 1024], P('pair', 'virt')
The draws below stay inside these ranges and needn't reach their ends.
Inputs may be any that keep to these rules, and one draw needn't show every extreme that they name: `mask_amp`: 1 marks an amplitude tile that is kept, 0 one that is screened out. `mask_int`: 1 marks an integral tile that is kept, 0 one that is screened out.
All inputs are finite; a program needn't handle non-finite values. No bound on the sum of `mask_int` on one device may be relied on, other than what follows from the above.
Results may differ from the reference program's by a relative error of at most 0.001.
Values may be sent and summed in bfloat16 or wider, within the bound.
No kernel may reach another device: no remote copies, remote signals or barrier semaphores. Data moves between devices by JAX's collectives and lax.ppermute only.
A program may use at most 64 MiB of HBM per device.

```python
import jax
import jax.numpy as jnp
from jax import lax

TILE_SIZE = 128
SLAB_TILES = 8
PAIR_ROWS = 14336
ROW_TILES = 112
CONTRACT_TILES = 512
CONTRACT_WIDTH = 65536
SLAB_WIDTH = 1024


def draw_mask_amp(key, part):
    key = jax.random.fold_in(key, 11)
    scores = jax.random.randint(key, (ROW_TILES, CONTRACT_TILES), 0, 1000)
    column = jnp.arange(CONTRACT_TILES, dtype=jnp.int32)
    limit = 250 + 500 * column // max(CONTRACT_TILES - 1, 1)
    return (scores < limit[None, :]).astype(jnp.int32)


def touch_ends(values, rng, smallest, largest):
    place = [jax.random.randint(jax.random.fold_in(rng, axis), (), 0, length) for axis, length in enumerate(values.shape)]
    main_axis = values.shape.index(max(values.shape))
    beside = place[:main_axis] + [(place[main_axis] + 1) % values.shape[main_axis]] + place[main_axis + 1:]
    return values.at[tuple(place)].set(smallest).at[tuple(beside)].set(largest)


def spiked(drawn, own_key, source, target, blocks, factor):
    owner, partner = [(jnp.arange(drawn.shape[position]) // (drawn.shape[position] // blocks)).reshape([-1 if axis == position else 1 for axis in range(drawn.ndim)]) for position in (source, target)]
    chosen = jax.random.permutation(own_key, blocks)[partner]
    strong = (owner == chosen) | (owner == (partner + blocks // 2) % blocks)
    return jnp.where(strong, factor * drawn, drawn)


def steps_of(own_key, extent, cuts, smallest, top_value):
    factor_of, own = 1.0, jax.random.fold_in(own_key, 6)
    for position, parts in cuts:
        draws = jnp.exp(jax.random.uniform(jax.random.fold_in(own, position), (parts,), jnp.float32, smallest / len(cuts), top_value / len(cuts)))
        factor_of = factor_of * jnp.repeat(draws, extent[position] // parts).reshape([-1 if axis == position else 1 for axis in range(len(extent))])
    return factor_of


def centred(stream_key, extent, width, most, cuts=(), kind=jnp.bfloat16):
    values = jax.random.normal(stream_key, extent, jnp.float32) * width
    if len(cuts) > 0:
        values = steps_of(stream_key, extent, cuts, -0.22, 0.18) * values
    return jnp.clip(values, min=-most, max=most).astype(kind)


def bell_draw_with(stream_key, shape, spread, most, shards, heavy, held_as=jnp.bfloat16):
    values = spread * jax.random.normal(stream_key, shape, jnp.float32)
    if shards:
        values = values * steps_of(stream_key, shape, shards, -0.22, 0.18)
    return jnp.clip(spiked(values, jax.random.fold_in(stream_key, 3), *heavy), -most, most).astype(held_as)


def setup_inputs(seed: int = 0) -> dict:
    splits = jax.random.split(jax.random.key(seed), 5)
    return {
        "amplitudes": centred(splits[0], (PAIR_ROWS, CONTRACT_WIDTH), 1.0, 6.0, ((0, 16), (1, 32))),
        "mask_amp": draw_mask_amp(jax.random.fold_in(splits[4], 71), 0),
        "integrals": bell_draw_with(splits[2], (CONTRACT_WIDTH, SLAB_WIDTH), (CONTRACT_WIDTH // 4) ** -0.5, 0.09375, ((0, 32), (1, 16)), (0, 1, 32, 2.75)),
        "mask_int": touch_ends((jax.random.randint(splits[3], (CONTRACT_TILES, SLAB_TILES), 0, 2) < 1).astype(jnp.int32), jax.random.fold_in(splits[3], 1), 0, 1),
    }


def reference(amplitudes, mask_amp, integrals, mask_int):
    edge_len = TILE_SIZE
    int_mask = jnp.repeat(jnp.repeat(mask_int, edge_len, axis=0), edge_len, axis=1).astype(integrals.dtype)
    int_kept = integrals * int_mask

    def row_block(pieces):
        block_rows, mask_row = pieces
        amp_mask = jnp.repeat(mask_row, edge_len).astype(block_rows.dtype)
        amp_kept = block_rows * amp_mask[None, :]
        return jnp.dot(amp_kept, int_kept, preferred_element_type=jnp.float32).astype(jnp.bfloat16)

    blocks = amplitudes.reshape(ROW_TILES, edge_len, CONTRACT_WIDTH)
    result = lax.map(row_block, (blocks, mask_amp))
    return result.reshape(PAIR_ROWS, SLAB_WIDTH)
```

```python
import jax
import jax.numpy as jnp
from jax import lax
from jax.sharding import Mesh, PartitionSpec as P

TILE_SIZE = 128
PLANE = ("y", "x")
LEVELS = 7
LIFT = 2.0**16
FIRST_SCALE = 2.0**18
FIRST_LIMIT = 2.0**-19


def column_levels(largest):
    level = jnp.zeros_like(largest)
    for step in range(LEVELS - 1):
        level = jnp.where(largest < FIRST_LIMIT * LIFT**-step, step + 1.0, level)
    return level


def of_level(level, sign):
    value = jnp.full_like(level, FIRST_SCALE**sign)
    for step in range(1, LEVELS):
        value = jnp.where(level == step, (FIRST_SCALE * LIFT**step) ** sign, value)
    return value


def shards(amplitudes, mask_amp, integrals, mask_int):
    row_tiles, depth_tiles = mask_amp.shape
    depth, width = integrals.shape
    half = width // 2
    pair, core = lax.axis_index("pair"), lax.axis_index("core")
    other = [(0, 1), (1, 0)]

    kept = lax.dynamic_slice_in_dim(mask_int, pair * width // TILE_SIZE, 1, 1)[:, 0]
    columns = integrals.T.astype(jnp.float32).reshape(width, depth_tiles, TILE_SIZE)
    columns = (columns * kept.astype(jnp.float32)[None, :, None]).reshape(width, depth)
    level = column_levels(jnp.max(jnp.abs(columns), axis=1, keepdims=True))
    coded = (columns * of_level(level, 1)).astype(jnp.float16)
    coded = jnp.concatenate(
        [coded, jnp.broadcast_to(level, (width, TILE_SIZE)).astype(jnp.float16)], axis=1
    )
    mine = lax.dynamic_slice_in_dim(coded, core * half, half, 0)
    theirs = lax.ppermute(lax.dynamic_slice_in_dim(coded, (1 - core) * half, half, 0), "core", other)

    amp_mask = mask_amp.astype(jnp.bfloat16)
    amp_kept = (
        amplitudes.reshape(row_tiles, TILE_SIZE, depth_tiles, TILE_SIZE) * amp_mask[:, None, :, None]
    ).reshape(amplitudes.shape)
    amp_theirs = lax.ppermute(amp_kept, "core", other)

    sent = jnp.concatenate(
        [mine[:, :depth], theirs[:, :depth], mine[:, depth : depth + 64], theirs[:, depth : depth + 64]],
        axis=1,
    )
    slab = lax.all_gather(sent, "pair", axis=0, tiled=True)

    def product(start, level_at, amps):
        block = slab[:, start : start + depth].astype(jnp.bfloat16)
        scale = of_level(slab[:, level_at : level_at + 1].astype(jnp.float32), -1)
        return scale * lax.dot_general(
            block, amps, (((1,), (1,)), ((), ())), preferred_element_type=jnp.float32
        )

    partial_value = product(0, 2 * depth, amp_kept) + product(depth, 2 * depth + 64, amp_theirs)
    pieces = lax.all_to_all(partial_value, PLANE, 0, 0, tiled=True)
    total = jnp.sum(pieces.reshape(-1, half, pieces.shape[1]), axis=0)
    return total.astype(jnp.bfloat16).T


def solution(mesh):
    grid = Mesh(mesh.devices.reshape(-1, 4, 4, 2), ("pair", "y", "x", "core"))
    virt = ("y", "x", "core")
    return jax.shard_map(
        shards,
        mesh=grid,
        in_specs=(P("pair", virt), P("pair", virt), P(virt, "pair"), P(virt, None)),
        out_specs=P("pair", virt),
        check_vma=False,
    )
```

```python
import jax
import jax.numpy as jnp
from jax import lax
from jax.experimental import pallas as pl
from jax.experimental.pallas import tpu as pltpu
from jax.sharding import Mesh, PartitionSpec as P

TILE_SIZE = 128
PLANE = ("y", "x")
OTHER_CORE = [(0, 1), (1, 0)]
LEVELS = 7
LIFT = 2.0**16
FIRST_SCALE = 2.0**18
FIRST_LIMIT = 2.0**-19


def column_levels(largest):
    level = jnp.zeros_like(largest)
    for step in range(LEVELS - 1):
        level = jnp.where(largest < FIRST_LIMIT * LIFT**-step, step + 1.0, level)
    return level


def of_level(level, sign):
    value = jnp.full_like(level, FIRST_SCALE**sign)
    for step in range(1, LEVELS):
        value = jnp.where(level == step, (FIRST_SCALE * LIFT**step) ** sign, value)
    return value


def lowered(steps):
    value = jnp.ones_like(steps)
    for step in range(1, LEVELS):
        value = jnp.where(steps == step, LIFT**-step, value)
    return value


def prepared(columns_ref, keep_amp_ref, keep_ref, stay_ref, away_ref, kept_ref, tail_ref):
    width, depth = columns_ref.shape
    half = width // 2
    slab = lax.axis_index("pair") // (TILE_SIZE // width)
    first = lax.axis_index("core") == 0
    largest = jnp.zeros((width, TILE_SIZE), jnp.float32)
    for tile in range(depth // TILE_SIZE):
        at = slice(tile * TILE_SIZE, (tile + 1) * TILE_SIZE)
        block = columns_ref[:, at].astype(jnp.float32) * keep_ref[slab, tile].astype(jnp.float32)
        kept_ref[:, at] = block
        largest = jnp.maximum(largest, jnp.abs(block))
    level = column_levels(jnp.max(largest, axis=1, keepdims=True))
    scaled = kept_ref[...] * of_level(level, 1)
    lower, upper = scaled[:half], scaled[half:]
    stay_ref[:, :depth] = jnp.where(first, lower, upper).astype(jnp.bfloat16)
    away_ref[:, :depth] = jnp.where(first, upper, lower).astype(jnp.bfloat16)
    level = jnp.broadcast_to(level, (width, TILE_SIZE))
    lower, upper = level[:half], level[half:]
    stay_ref[:, depth:] = jnp.where(first, lower, upper).astype(jnp.bfloat16)
    away_ref[:, depth : depth + TILE_SIZE] = jnp.where(first, upper, lower).astype(jnp.bfloat16)
    tail_ref[...] = jnp.zeros_like(tail_ref)
    tail_ref[: keep_amp_ref.shape[0], : keep_amp_ref.shape[1]] = keep_amp_ref[...].astype(jnp.float32)
    away_ref[:, depth + TILE_SIZE :] = tail_ref[...].astype(jnp.bfloat16)


def masked_product(columns_ref, mine_ref, theirs_ref, keep_mine_ref, keep_theirs_ref, out_ref, kept_ref, sems):
    depth = mine_ref.shape[1]
    loads = [
        pltpu.make_async_copy(amps, kept_ref.at[part], sems.at[part]) for part, amps in enumerate((mine_ref, theirs_ref))
    ]
    for load in loads:
        load.start()
    scale = of_level(columns_ref[:, 2 * depth : 2 * depth + 1].astype(jnp.float32), -1)
    for part, keep in enumerate((keep_mine_ref, keep_theirs_ref)):
        loads[part].wait()
        for row_tile in range(keep.shape[0]):
            for tile in range(keep.shape[1]):
                rows = slice(row_tile * TILE_SIZE, (row_tile + 1) * TILE_SIZE)
                at = slice(tile * TILE_SIZE, (tile + 1) * TILE_SIZE)
                kept_ref[part, rows, at] *= keep[row_tile, tile].astype(jnp.bfloat16)
    out_ref[...] = scale * sum(
        lax.dot_general(
            columns_ref[:, part * depth : (part + 1) * depth],
            kept_ref[part],
            (((1,), (1,)), ((), ())),
            preferred_element_type=jnp.float32,
        )
        for part in range(2)
    )


def shards(amplitudes, mask_amp, integrals, mask_int):
    row_tiles, depth_tiles = mask_amp.shape
    rows = amplitudes.shape[0]
    depth, width = integrals.shape
    half = width // 2

    vmem, smem = pl.BlockSpec(memory_space=pltpu.VMEM), pl.BlockSpec(memory_space=pltpu.SMEM)
    hbm = pl.BlockSpec(memory_space=pltpu.HBM)
    stay, away = pl.pallas_call(
        prepared,
        out_shape=(
            pltpu.VMEM((half, depth + TILE_SIZE), jnp.bfloat16),
            pltpu.VMEM((half, depth + 2 * TILE_SIZE), jnp.bfloat16),
        ),
        in_specs=[vmem, vmem, smem],
        out_specs=(vmem, vmem),
        scratch_shapes=[
            pltpu.VMEM((width, depth), jnp.float32),
            pltpu.VMEM((half, TILE_SIZE), jnp.float32),
        ],
    )(integrals.T, mask_amp, mask_int.T)
    theirs = lax.ppermute(away, "core", OTHER_CORE)
    amplitudes, stay = lax.optimization_barrier((amplitudes, stay))
    amp_theirs = lax.ppermute(amplitudes, "core", OTHER_CORE)
    keep_at = depth + TILE_SIZE
    keep_theirs = theirs[:row_tiles, keep_at : keep_at + depth_tiles].astype(jnp.int32)

    levels = [part[:, depth : depth + 1].astype(jnp.float32) for part in (stay, theirs)]
    level = jnp.minimum(*levels)
    sent = jnp.concatenate(
        [part[:, :depth].astype(jnp.float32) * lowered(own - level) for part, own in zip((stay, theirs), levels)]
        + [jnp.broadcast_to(level, (half, TILE_SIZE))],
        axis=1,
    ).astype(jnp.float16)
    columns = lax.all_gather(sent, "pair", axis=0, tiled=True).astype(jnp.bfloat16)

    partial_value = pl.pallas_call(
        masked_product,
        out_shape=jax.ShapeDtypeStruct((columns.shape[0], rows), jnp.float32),
        in_specs=[vmem, hbm, hbm, smem, smem],
        out_specs=vmem,
        scratch_shapes=[
            pltpu.VMEM((2, rows, depth), jnp.bfloat16),
            pltpu.SemaphoreType.DMA((2,)),
        ],
        compiler_params=pltpu.CompilerParams(vmem_limit_bytes=32 * 1024 * 1024),
        cost_estimate=pl.CostEstimate(
            flops=4 * columns.shape[0] * rows * depth, bytes_accessed=16 * 1024 * 1024, transcendentals=0
        ),
    )(columns, amplitudes, amp_theirs, mask_amp, keep_theirs)
    pieces = lax.all_to_all(partial_value, PLANE, 0, 0, tiled=True)
    total = jnp.sum(pieces.reshape(-1, half, pieces.shape[1]), axis=0)
    return total.astype(jnp.bfloat16).T


def solution(mesh):
    grid = Mesh(mesh.devices.reshape(-1, 4, 4, 2), ("pair", "y", "x", "core"))
    virt = ("y", "x", "core")
    return jax.shard_map(
        shards,
        mesh=grid,
        in_specs=(P("pair", virt), P("pair", virt), P(virt, "pair"), P(virt, None)),
        out_specs=P("pair", virt),
        check_vma=False,
    )
```

```python
import jax
import jax.numpy as jnp
from jax import lax
from jax.experimental import pallas as pl
from jax.experimental.pallas import tpu as pltpu
from jax.sharding import Mesh, PartitionSpec as P

TILE_SIZE = 128
PLANE = ("y", "x")
OTHER_CORE = [(0, 1), (1, 0)]
LEVELS = 7
LIFT = 2.0**16
FIRST_SCALE = 2.0**18
FIRST_LIMIT = 2.0**-19
STEPS = 32000.0
OCTAVE = 8.0
CODE_ROWS = 16
SMALLEST = 1e-33


def column_levels(largest):
    level = jnp.zeros_like(largest)
    for step in range(LEVELS - 1):
        level = jnp.where(largest < FIRST_LIMIT * LIFT**-step, step + 1.0, level)
    return level


def of_level(level, sign):
    value = jnp.full_like(level, FIRST_SCALE**sign)
    for step in range(1, LEVELS):
        value = jnp.where(level == step, (FIRST_SCALE * LIFT**step) ** sign, value)
    return value


def lowered(steps):
    value = jnp.ones_like(steps)
    for step in range(1, LEVELS):
        value = jnp.where(steps == step, LIFT**-step, value)
    return value


def prepared(columns_ref, keep_amp_ref, keep_ref, stay_ref, away_ref, kept_ref, tail_ref):
    width, depth = columns_ref.shape
    half = width // 2
    slab = lax.axis_index("pair") // (TILE_SIZE // width)
    first = lax.axis_index("core") == 0
    largest = jnp.zeros((width, TILE_SIZE), jnp.float32)
    for tile in range(depth // TILE_SIZE):
        at = slice(tile * TILE_SIZE, (tile + 1) * TILE_SIZE)
        block = columns_ref[:, at].astype(jnp.float32) * keep_ref[slab, tile].astype(jnp.float32)
        kept_ref[:, at] = block
        largest = jnp.maximum(largest, jnp.abs(block))
    level = column_levels(jnp.max(largest, axis=1, keepdims=True))
    scaled = kept_ref[...] * of_level(level, 1)
    lower, upper = scaled[:half], scaled[half:]
    stay_ref[:, :depth] = jnp.where(first, lower, upper).astype(jnp.bfloat16)
    away_ref[:, :depth] = jnp.where(first, upper, lower).astype(jnp.bfloat16)
    level = jnp.broadcast_to(level, (width, TILE_SIZE))
    lower, upper = level[:half], level[half:]
    stay_ref[:, depth:] = jnp.where(first, lower, upper).astype(jnp.bfloat16)
    away_ref[:, depth : depth + TILE_SIZE] = jnp.where(first, upper, lower).astype(jnp.bfloat16)
    tail_ref[...] = jnp.zeros_like(tail_ref)
    tail_ref[: keep_amp_ref.shape[0], : keep_amp_ref.shape[1]] = keep_amp_ref[...].astype(jnp.float32)
    away_ref[:, depth + TILE_SIZE :] = tail_ref[...].astype(jnp.bfloat16)


def masked_product(
    columns_ref, mine_ref, theirs_ref, keep_mine_ref, keep_theirs_ref, out_ref, kept_ref, total_ref, code_ref, sems
):
    depth = mine_ref.shape[1]
    loads = [
        pltpu.make_async_copy(amps, kept_ref.at[part], sems.at[part]) for part, amps in enumerate((mine_ref, theirs_ref))
    ]
    for load in loads:
        load.start()
    scale = of_level(columns_ref[:, 2 * depth : 2 * depth + 1].astype(jnp.float32), -1)
    for part, keep in enumerate((keep_mine_ref, keep_theirs_ref)):
        loads[part].wait()
        for row_tile in range(keep.shape[0]):
            for tile in range(keep.shape[1]):
                rows = slice(row_tile * TILE_SIZE, (row_tile + 1) * TILE_SIZE)
                at = slice(tile * TILE_SIZE, (tile + 1) * TILE_SIZE)
                kept_ref[part, rows, at] *= keep[row_tile, tile].astype(jnp.bfloat16)
    total_ref[...] = scale * sum(
        lax.dot_general(
            columns_ref[:, part * depth : (part + 1) * depth],
            kept_ref[part],
            (((1,), (1,)), ((), ())),
            preferred_element_type=jnp.float32,
        )
        for part in range(2)
    )
    pieces, row_tiles = out_ref.shape[0], keep_mine_ref.shape[0]
    half = columns_ref.shape[0] // pieces

    def block(piece, tile):
        return total_ref[piece * half : (piece + 1) * half, tile * TILE_SIZE : (tile + 1) * TILE_SIZE]

    code_ref[...] = jnp.zeros_like(code_ref)
    for piece in range(pieces):
        for tile in range(row_tiles):
            largest = jnp.max(jnp.abs(block(piece, tile)), axis=0, keepdims=True)
            code_ref[piece * CODE_ROWS + tile : piece * CODE_ROWS + tile + 1, :] = largest
    codes = jnp.ceil(jnp.log2(jnp.maximum(code_ref[...], SMALLEST) / STEPS) * OCTAVE)
    code_ref[...] = jnp.exp2(codes * (-1.0 / OCTAVE))
    codes = codes.astype(jnp.int32).astype(jnp.int16)
    for piece in range(pieces):
        for tile in range(row_tiles):
            inverse = code_ref[piece * CODE_ROWS + tile : piece * CODE_ROWS + tile + 1, :]
            fixed = jnp.round(block(piece, tile) * inverse).astype(jnp.int32).astype(jnp.int16)
            out_ref[piece, tile * half : (tile + 1) * half, :] = fixed
        out_ref[piece, row_tiles * half :, :] = codes[piece * CODE_ROWS : (piece + 1) * CODE_ROWS]


def shards(amplitudes, mask_amp, integrals, mask_int):
    row_tiles, depth_tiles = mask_amp.shape
    rows = amplitudes.shape[0]
    depth, width = integrals.shape
    half = width // 2

    vmem, smem = pl.BlockSpec(memory_space=pltpu.VMEM), pl.BlockSpec(memory_space=pltpu.SMEM)
    hbm = pl.BlockSpec(memory_space=pltpu.HBM)
    stay, away = pl.pallas_call(
        prepared,
        out_shape=(
            pltpu.VMEM((half, depth + TILE_SIZE), jnp.bfloat16),
            pltpu.VMEM((half, depth + 2 * TILE_SIZE), jnp.bfloat16),
        ),
        in_specs=[vmem, vmem, smem],
        out_specs=(vmem, vmem),
        scratch_shapes=[
            pltpu.VMEM((width, depth), jnp.float32),
            pltpu.VMEM((half, TILE_SIZE), jnp.float32),
        ],
    )(integrals.T, mask_amp, mask_int.T)
    theirs = lax.ppermute(away, "core", OTHER_CORE)
    amplitudes, stay = lax.optimization_barrier((amplitudes, stay))
    amp_theirs = lax.ppermute(amplitudes, "core", OTHER_CORE)
    keep_at = depth + TILE_SIZE
    keep_theirs = theirs[:row_tiles, keep_at : keep_at + depth_tiles].astype(jnp.int32)

    levels = [part[:, depth : depth + 1].astype(jnp.float32) for part in (stay, theirs)]
    level = jnp.minimum(*levels)
    sent = jnp.concatenate(
        [part[:, :depth].astype(jnp.float32) * lowered(own - level) for part, own in zip((stay, theirs), levels)]
        + [jnp.broadcast_to(level, (half, TILE_SIZE))],
        axis=1,
    ).astype(jnp.float16)
    columns = lax.all_gather(sent, "pair", axis=0, tiled=True).astype(jnp.bfloat16)

    pieces = columns.shape[0] // half
    partial_value = pl.pallas_call(
        masked_product,
        out_shape=jax.ShapeDtypeStruct((pieces, row_tiles * half + CODE_ROWS, TILE_SIZE), jnp.int16),
        in_specs=[vmem, hbm, hbm, smem, smem],
        out_specs=vmem,
        scratch_shapes=[
            pltpu.VMEM((2, rows, depth), jnp.bfloat16),
            pltpu.VMEM((columns.shape[0], rows), jnp.float32),
            pltpu.VMEM((pieces * CODE_ROWS, TILE_SIZE), jnp.float32),
            pltpu.SemaphoreType.DMA((2,)),
        ],
        compiler_params=pltpu.CompilerParams(vmem_limit_bytes=32 * 1024 * 1024),
        cost_estimate=pl.CostEstimate(
            flops=4 * columns.shape[0] * rows * depth, bytes_accessed=16 * 1024 * 1024, transcendentals=0
        ),
    )(columns, amplitudes, amp_theirs, mask_amp, keep_theirs)
    partial_value = lax.all_to_all(partial_value, PLANE, 0, 0, tiled=True).astype(jnp.float32)
    steps = jnp.exp2(partial_value[:, row_tiles * half : row_tiles * half + row_tiles] * (1.0 / OCTAVE))
    fixed = partial_value[:, : row_tiles * half].reshape(pieces, row_tiles, half, TILE_SIZE)
    total = jnp.sum(fixed * steps[:, :, None, :], axis=0)
    return total.astype(jnp.bfloat16).transpose(0, 2, 1).reshape(rows, half)


def solution(mesh):
    grid = Mesh(mesh.devices.reshape(-1, 4, 4, 2), ("pair", "y", "x", "core"))
    virt = ("y", "x", "core")
    return jax.shard_map(
        shards,
        mesh=grid,
        in_specs=(P("pair", virt), P("pair", virt), P(virt, "pair"), P(virt, None)),
        out_specs=P("pair", virt),
        check_vma=False,
    )
```

```python
import jax
import jax.numpy as jnp
from jax import lax
from jax.experimental import pallas as pl
from jax.experimental.pallas import tpu as pltpu
from jax.sharding import Mesh, PartitionSpec as P

TILE_SIZE = 128
PLANE = ("y", "x")
OTHER_CORE = [(0, 1), (1, 0)]
LEVELS = 7
LIFT = 2.0**16
FIRST_SCALE = 2.0**18
FIRST_LIMIT = 2.0**-19
STEPS = 32000.0
OCTAVE = 8.0
CODE_ROWS = 16
SMALLEST = 1e-33


def column_levels(largest):
    level = jnp.zeros_like(largest)
    for step in range(LEVELS - 1):
        level = jnp.where(largest < FIRST_LIMIT * LIFT**-step, step + 1.0, level)
    return level


def of_level(level, sign):
    value = jnp.full_like(level, FIRST_SCALE**sign)
    for step in range(1, LEVELS):
        value = jnp.where(level == step, (FIRST_SCALE * LIFT**step) ** sign, value)
    return value


def lowered(steps):
    value = jnp.ones_like(steps)
    for step in range(1, LEVELS):
        value = jnp.where(steps == step, LIFT**-step, value)
    return value


def prepared(columns_ref, keep_amp_ref, keep_ref, stay_ref, away_ref, kept_ref, tail_ref):
    width, depth = columns_ref.shape
    half = width // 2
    slab = lax.axis_index("pair") // (TILE_SIZE // width)
    first = lax.axis_index("core") == 0
    largest = jnp.zeros((width, TILE_SIZE), jnp.float32)
    for tile in range(depth // TILE_SIZE):
        at = slice(tile * TILE_SIZE, (tile + 1) * TILE_SIZE)
        block = columns_ref[:, at].astype(jnp.float32) * keep_ref[slab, tile].astype(jnp.float32)
        kept_ref[:, at] = block
        largest = jnp.maximum(largest, jnp.abs(block))
    level = column_levels(jnp.max(largest, axis=1, keepdims=True))
    scaled = kept_ref[...] * of_level(level, 1)
    lower, upper = scaled[:half], scaled[half:]
    stay_ref[:, :depth] = jnp.where(first, lower, upper).astype(jnp.bfloat16)
    away_ref[:, :depth] = jnp.where(first, upper, lower).astype(jnp.bfloat16)
    level = jnp.broadcast_to(level, (width, TILE_SIZE))
    lower, upper = level[:half], level[half:]
    stay_ref[:, depth:] = jnp.where(first, lower, upper).astype(jnp.bfloat16)
    away_ref[:, depth : depth + TILE_SIZE] = jnp.where(first, upper, lower).astype(jnp.bfloat16)
    tail_ref[...] = jnp.zeros_like(tail_ref)
    tail_ref[: keep_amp_ref.shape[0], : keep_amp_ref.shape[1]] = keep_amp_ref[...].astype(jnp.float32)
    away_ref[:, depth + TILE_SIZE :] = tail_ref[...].astype(jnp.bfloat16)


def fixed_point(near_ref, far_ref, level_ref, out_ref, total_ref, code_ref):
    total_ref[...] = of_level(level_ref[:, :1].astype(jnp.float32), -1) * (near_ref[...] + far_ref[...])
    pieces, half = out_ref.shape[0], near_ref.shape[0] // out_ref.shape[0]
    row_tiles = near_ref.shape[1] // TILE_SIZE

    def block(piece, tile):
        return total_ref[piece * half : (piece + 1) * half, tile * TILE_SIZE : (tile + 1) * TILE_SIZE]

    code_ref[...] = jnp.zeros_like(code_ref)
    for piece in range(pieces):
        for tile in range(row_tiles):
            largest = jnp.max(jnp.abs(block(piece, tile)), axis=0, keepdims=True)
            code_ref[piece * CODE_ROWS + tile : piece * CODE_ROWS + tile + 1, :] = largest
    codes = jnp.ceil(jnp.log2(jnp.maximum(code_ref[...], SMALLEST) / STEPS) * OCTAVE)
    code_ref[...] = jnp.exp2(codes * (-1.0 / OCTAVE))
    codes = codes.astype(jnp.int32).astype(jnp.int16)
    for piece in range(pieces):
        for tile in range(row_tiles):
            inverse = code_ref[piece * CODE_ROWS + tile : piece * CODE_ROWS + tile + 1, :]
            fixed = jnp.round(block(piece, tile) * inverse).astype(jnp.int32).astype(jnp.int16)
            out_ref[piece, tile * half : (tile + 1) * half, :] = fixed
        out_ref[piece, row_tiles * half :, :] = codes[piece * CODE_ROWS : (piece + 1) * CODE_ROWS]


def shards(amplitudes, mask_amp, integrals, mask_int):
    row_tiles, depth_tiles = mask_amp.shape
    rows = amplitudes.shape[0]
    depth, width = integrals.shape
    half = width // 2

    vmem, smem = pl.BlockSpec(memory_space=pltpu.VMEM), pl.BlockSpec(memory_space=pltpu.SMEM)
    stay, away = pl.pallas_call(
        prepared,
        out_shape=(
            pltpu.VMEM((half, depth + TILE_SIZE), jnp.bfloat16),
            pltpu.VMEM((half, depth + 2 * TILE_SIZE), jnp.bfloat16),
        ),
        in_specs=[vmem, vmem, smem],
        out_specs=(vmem, vmem),
        scratch_shapes=[
            pltpu.VMEM((width, depth), jnp.float32),
            pltpu.VMEM((half, TILE_SIZE), jnp.float32),
        ],
    )(integrals.T, mask_amp, mask_int.T)
    theirs = lax.ppermute(away, "core", OTHER_CORE)
    amplitudes, stay = lax.optimization_barrier((amplitudes, stay))
    amp_theirs = lax.ppermute(amplitudes, "core", OTHER_CORE)
    keep_at = depth + TILE_SIZE
    keep_mine, keep_theirs = (part[:row_tiles, keep_at : keep_at + depth_tiles] for part in (away, theirs))

    levels = [part[:, depth : depth + 1].astype(jnp.float32) for part in (stay, theirs)]
    level = jnp.minimum(*levels)
    sent = jnp.concatenate(
        [part[:, :depth].astype(jnp.float32) * lowered(own - level) for part, own in zip((stay, theirs), levels)]
        + [jnp.broadcast_to(level, (half, TILE_SIZE))],
        axis=1,
    ).astype(jnp.float16)
    columns = lax.all_gather(sent, "pair", axis=0, tiled=True).astype(jnp.bfloat16)

    def product(columns, amps, keep):
        keep = lax.optimization_barrier(jnp.repeat(keep, TILE_SIZE, axis=1))
        amp_kept = (amps.reshape(row_tiles, TILE_SIZE, depth) * keep[:, None, :]).reshape(amps.shape)
        return lax.dot_general(columns, amp_kept, (((1,), (1,)), ((), ())), preferred_element_type=jnp.float32)

    far = product(columns[:, depth : 2 * depth], amp_theirs, keep_theirs)
    columns, far, keep_mine = lax.optimization_barrier((columns, far, keep_mine))
    near = product(columns[:, :depth], amplitudes, keep_mine)
    pieces = columns.shape[0] // half
    partial_value = pl.pallas_call(
        fixed_point,
        out_shape=jax.ShapeDtypeStruct((pieces, row_tiles * half + CODE_ROWS, TILE_SIZE), jnp.int16),
        in_specs=[vmem, vmem, vmem],
        out_specs=vmem,
        scratch_shapes=[
            pltpu.VMEM((columns.shape[0], rows), jnp.float32),
            pltpu.VMEM((pieces * CODE_ROWS, TILE_SIZE), jnp.float32),
        ],
        compiler_params=pltpu.CompilerParams(vmem_limit_bytes=16 * 1024 * 1024),
    )(near, far, columns[:, 2 * depth :])
    partial_value = lax.all_to_all(partial_value, PLANE, 0, 0, tiled=True).astype(jnp.float32)
    steps = jnp.exp2(partial_value[:, row_tiles * half : row_tiles * half + row_tiles] * (1.0 / OCTAVE))
    fixed = partial_value[:, : row_tiles * half].reshape(pieces, row_tiles, half, TILE_SIZE)
    total = jnp.sum(fixed * steps[:, :, None, :], axis=0)
    return total.astype(jnp.bfloat16).transpose(0, 2, 1).reshape(rows, half)


def solution(mesh):
    grid = Mesh(mesh.devices.reshape(-1, 4, 4, 2), ("pair", "y", "x", "core"))
    virt = ("y", "x", "core")
    return jax.shard_map(
        shards,
        mesh=grid,
        in_specs=(P("pair", virt), P("pair", virt), P(virt, "pair"), P(virt, None)),
        out_specs=P("pair", virt),
        check_vma=False,
    )
```

```python
import jax
import jax.numpy as jnp
from jax import lax
from jax.experimental import pallas as pl
from jax.experimental.pallas import tpu as pltpu
from jax.sharding import Mesh, PartitionSpec as P

TILE_SIZE = 128
PLANE = ("y", "x")
OTHER_CORE = [(0, 1), (1, 0)]
LEVELS = 7
LIFT = 2.0**16
FIRST_SCALE = 2.0**18
FIRST_LIMIT = 2.0**-19


def column_levels(largest):
    level = jnp.zeros_like(largest)
    for step in range(LEVELS - 1):
        level = jnp.where(largest < FIRST_LIMIT * LIFT**-step, step + 1.0, level)
    return level


def of_level(level, sign):
    value = jnp.full_like(level, FIRST_SCALE**sign)
    for step in range(1, LEVELS):
        value = jnp.where(level == step, (FIRST_SCALE * LIFT**step) ** sign, value)
    return value


def lowered(steps):
    value = jnp.ones_like(steps)
    for step in range(1, LEVELS):
        value = jnp.where(steps == step, LIFT**-step, value)
    return value


def prepared(columns_ref, keep_amp_ref, keep_ref, stay_ref, away_ref, kept_ref, tail_ref):
    width, depth = columns_ref.shape
    half = width // 2
    slab = lax.axis_index("pair") // (TILE_SIZE // width)
    first = lax.axis_index("core") == 0
    largest = jnp.zeros((width, TILE_SIZE), jnp.float32)
    for tile in range(depth // TILE_SIZE):
        at = slice(tile * TILE_SIZE, (tile + 1) * TILE_SIZE)
        block = columns_ref[:, at].astype(jnp.float32) * keep_ref[slab, tile].astype(jnp.float32)
        kept_ref[:, at] = block
        largest = jnp.maximum(largest, jnp.abs(block))
    level = column_levels(jnp.max(largest, axis=1, keepdims=True))
    scaled = kept_ref[...] * of_level(level, 1)
    lower, upper = scaled[:half], scaled[half:]
    stay_ref[:, :depth] = jnp.where(first, lower, upper).astype(jnp.bfloat16)
    away_ref[:, :depth] = jnp.where(first, upper, lower).astype(jnp.bfloat16)
    level = jnp.broadcast_to(level, (width, TILE_SIZE))
    lower, upper = level[:half], level[half:]
    stay_ref[:, depth:] = jnp.where(first, lower, upper).astype(jnp.bfloat16)
    away_ref[:, depth : depth + TILE_SIZE] = jnp.where(first, upper, lower).astype(jnp.bfloat16)
    tail_ref[...] = jnp.zeros_like(tail_ref)
    tail_ref[: keep_amp_ref.shape[0], : keep_amp_ref.shape[1]] = keep_amp_ref[...].astype(jnp.float32)
    away_ref[:, depth + TILE_SIZE :] = tail_ref[...].astype(jnp.bfloat16)


def shards(amplitudes, mask_amp, integrals, mask_int):
    row_tiles, depth_tiles = mask_amp.shape
    rows = amplitudes.shape[0]
    depth, width = integrals.shape
    half = width // 2

    vmem, smem = pl.BlockSpec(memory_space=pltpu.VMEM), pl.BlockSpec(memory_space=pltpu.SMEM)
    stay, away = pl.pallas_call(
        prepared,
        out_shape=(
            pltpu.VMEM((half, depth + TILE_SIZE), jnp.bfloat16),
            pltpu.VMEM((half, depth + 2 * TILE_SIZE), jnp.bfloat16),
        ),
        in_specs=[vmem, vmem, smem],
        out_specs=(vmem, vmem),
        scratch_shapes=[
            pltpu.VMEM((width, depth), jnp.float32),
            pltpu.VMEM((half, TILE_SIZE), jnp.float32),
        ],
    )(integrals.T, mask_amp, mask_int.T)
    theirs = lax.ppermute(away, "core", OTHER_CORE)
    amplitudes, stay = lax.optimization_barrier((amplitudes, stay))
    amp_theirs = lax.ppermute(amplitudes, "core", OTHER_CORE)
    keep_at = depth + TILE_SIZE
    keep_mine, keep_theirs = (part[:row_tiles, keep_at : keep_at + depth_tiles] for part in (away, theirs))

    levels = [part[:, depth : depth + 1].astype(jnp.float32) for part in (stay, theirs)]
    level = jnp.minimum(*levels)
    sent = jnp.concatenate(
        [part[:, :depth].astype(jnp.float32) * lowered(own - level) for part, own in zip((stay, theirs), levels)]
        + [jnp.broadcast_to(level, (half, TILE_SIZE))],
        axis=1,
    ).astype(jnp.float16)
    columns = lax.all_gather(sent, "pair", axis=0, tiled=True).astype(jnp.bfloat16)

    def product(columns, amps, keep):
        keep = lax.optimization_barrier(jnp.repeat(keep, TILE_SIZE, axis=1))
        amp_kept = (amps.reshape(row_tiles, TILE_SIZE, depth) * keep[:, None, :]).reshape(amps.shape)
        return lax.dot_general(columns, amp_kept, (((1,), (1,)), ((), ())), preferred_element_type=jnp.float32)

    far = product(columns[:, depth : 2 * depth], amp_theirs, keep_theirs)
    columns, far, keep_mine = lax.optimization_barrier((columns, far, keep_mine))
    near = product(columns[:, :depth], amplitudes, keep_mine)
    scale = of_level(columns[:, 2 * depth : 2 * depth + 1].astype(jnp.float32), -1)
    near, far = lax.optimization_barrier((near, far))
    pieces = lax.all_to_all(scale * (near + far), PLANE, 0, 0, tiled=True)
    return jnp.sum(pieces.reshape(-1, half, rows), axis=0).astype(jnp.bfloat16).T


def solution(mesh):
    grid = Mesh(mesh.devices.reshape(-1, 4, 4, 2), ("pair", "y", "x", "core"))
    virt = ("y", "x", "core")
    return jax.shard_map(
        shards,
        mesh=grid,
        in_specs=(P("pair", virt), P("pair", virt), P(virt, "pair"), P(virt, None)),
        out_specs=P("pair", virt),
        check_vma=False,
    )
```

```python
import jax
import jax.numpy as jnp
from jax import lax
from jax.experimental import pallas as pl
from jax.experimental.pallas import tpu as pltpu
from jax.sharding import Mesh, PartitionSpec as P

TILE_SIZE = 128
PLANE = ("y", "x")
OTHER_CORE = [(0, 1), (1, 0)]
LEVELS = 7
LIFT = 2.0**16
FIRST_SCALE = 2.0**18
FIRST_LIMIT = 2.0**-19
TAIL = 64
STEPS = 32000.0
OCTAVE = 8.0
CODE_ROWS = 16
SMALLEST = 1e-33


def column_levels(largest):
    level = jnp.zeros_like(largest)
    for step in range(LEVELS - 1):
        level = jnp.where(largest < FIRST_LIMIT * LIFT**-step, step + 1.0, level)
    return level


def of_level(level, sign):
    value = jnp.full_like(level, FIRST_SCALE**sign)
    for step in range(1, LEVELS):
        value = jnp.where(level == step, (FIRST_SCALE * LIFT**step) ** sign, value)
    return value


def prepared(columns_ref, keep_amp_ref, keep_ref, stay_ref, away_ref, kept_ref, tail_ref):
    width, depth = columns_ref.shape
    half = width // 2
    slab = lax.axis_index("pair") // (TILE_SIZE // width)
    first = lax.axis_index("core") == 0
    largest = jnp.zeros((width, TILE_SIZE), jnp.float32)
    for tile in range(depth // TILE_SIZE):
        at = slice(tile * TILE_SIZE, (tile + 1) * TILE_SIZE)
        block = columns_ref[:, at].astype(jnp.float32) * keep_ref[slab, tile].astype(jnp.float32)
        kept_ref[:, at] = block
        largest = jnp.maximum(largest, jnp.abs(block))
    level = column_levels(jnp.max(largest, axis=1, keepdims=True))
    scaled = kept_ref[...] * of_level(level, 1)
    lower, upper = scaled[:half], scaled[half:]
    stay_ref[:, :depth] = jnp.where(first, lower, upper).astype(jnp.bfloat16)
    away_ref[:, :depth] = jnp.where(first, upper, lower).astype(jnp.bfloat16)
    level = jnp.broadcast_to(level, (width, TILE_SIZE))
    lower, upper = level[:half], level[half:]
    stay_ref[:, depth:] = jnp.where(first, lower, upper).astype(jnp.bfloat16)
    away_ref[:, depth : depth + TILE_SIZE] = jnp.where(first, upper, lower).astype(jnp.bfloat16)
    tail_ref[...] = jnp.zeros_like(tail_ref)
    tail_ref[: keep_amp_ref.shape[0], : keep_amp_ref.shape[1]] = keep_amp_ref[...].astype(jnp.float32)
    away_ref[:, depth + TILE_SIZE :] = tail_ref[...].astype(jnp.bfloat16)


def fixed_point(near_ref, far_ref, level_ref, out_ref, total_ref, code_ref):
    near_scale, far_scale = (
        of_level(level_ref[:, lane : lane + 1].astype(jnp.float32), -1) for lane in (0, TAIL)
    )
    total_ref[...] = near_scale * near_ref[...] + far_scale * far_ref[...]
    pieces, half = out_ref.shape[0], near_ref.shape[0] // out_ref.shape[0]
    row_tiles = near_ref.shape[1] // TILE_SIZE

    def block(piece, tile):
        return total_ref[piece * half : (piece + 1) * half, tile * TILE_SIZE : (tile + 1) * TILE_SIZE]

    code_ref[...] = jnp.zeros_like(code_ref)
    for piece in range(pieces):
        for tile in range(row_tiles):
            largest = jnp.max(jnp.abs(block(piece, tile)), axis=0, keepdims=True)
            code_ref[piece * CODE_ROWS + tile : piece * CODE_ROWS + tile + 1, :] = largest
    codes = jnp.ceil(jnp.log2(jnp.maximum(code_ref[...], SMALLEST) / STEPS) * OCTAVE)
    code_ref[...] = jnp.exp2(codes * (-1.0 / OCTAVE))
    codes = codes.astype(jnp.int32).astype(jnp.int16)
    for piece in range(pieces):
        for tile in range(row_tiles):
            inverse = code_ref[piece * CODE_ROWS + tile : piece * CODE_ROWS + tile + 1, :]
            fixed = jnp.round(block(piece, tile) * inverse).astype(jnp.int32).astype(jnp.int16)
            out_ref[piece, tile * half : (tile + 1) * half, :] = fixed
        out_ref[piece, row_tiles * half :, :] = codes[piece * CODE_ROWS : (piece + 1) * CODE_ROWS]


def shards(amplitudes, mask_amp, integrals, mask_int):
    row_tiles, depth_tiles = mask_amp.shape
    rows = amplitudes.shape[0]
    depth, width = integrals.shape
    half = width // 2

    vmem, smem = pl.BlockSpec(memory_space=pltpu.VMEM), pl.BlockSpec(memory_space=pltpu.SMEM)
    stay, away = pl.pallas_call(
        prepared,
        out_shape=(
            pltpu.VMEM((half, depth + TILE_SIZE), jnp.bfloat16),
            pltpu.VMEM((half, depth + 2 * TILE_SIZE), jnp.bfloat16),
        ),
        in_specs=[vmem, vmem, smem],
        out_specs=(vmem, vmem),
        scratch_shapes=[
            pltpu.VMEM((width, depth), jnp.float32),
            pltpu.VMEM((half, TILE_SIZE), jnp.float32),
        ],
    )(integrals.T, mask_amp, mask_int.T)
    theirs = lax.ppermute(away, "core", OTHER_CORE)
    amplitudes, stay = lax.optimization_barrier((amplitudes, stay))
    amp_theirs = lax.ppermute(amplitudes, "core", OTHER_CORE)
    keep_at = depth + TILE_SIZE
    keep_mine, keep_theirs = (part[:row_tiles, keep_at : keep_at + depth_tiles] for part in (away, theirs))

    stay, theirs = (part[:, : depth + TAIL].astype(jnp.float32) for part in (stay, theirs))
    theirs = lax.optimization_barrier(theirs)
    levels = lax.optimization_barrier(jnp.concatenate([part[:, depth:] for part in (stay, theirs)], axis=1))
    blocks = lax.optimization_barrier([part[:, :depth].astype(jnp.float16) for part in (stay, theirs)])
    sent = jnp.concatenate([*blocks, levels.astype(jnp.float16)], axis=1)
    columns = lax.all_gather(sent, "pair", axis=0, tiled=True).astype(jnp.bfloat16)

    def product(columns, amps, keep):
        keep = lax.optimization_barrier(jnp.repeat(keep, TILE_SIZE, axis=1))
        amp_kept = (amps.reshape(row_tiles, TILE_SIZE, depth) * keep[:, None, :]).reshape(amps.shape)
        return lax.dot_general(columns, amp_kept, (((1,), (1,)), ((), ())), preferred_element_type=jnp.float32)

    far = product(columns[:, depth : 2 * depth], amp_theirs, keep_theirs)
    columns, far, keep_mine = lax.optimization_barrier((columns, far, keep_mine))
    near = product(columns[:, :depth], amplitudes, keep_mine)
    pieces = columns.shape[0] // half
    partial_value = pl.pallas_call(
        fixed_point,
        out_shape=jax.ShapeDtypeStruct((pieces, row_tiles * half + CODE_ROWS, TILE_SIZE), jnp.int16),
        in_specs=[vmem, vmem, vmem],
        out_specs=vmem,
        scratch_shapes=[
            pltpu.VMEM((columns.shape[0], rows), jnp.float32),
            pltpu.VMEM((pieces * CODE_ROWS, TILE_SIZE), jnp.float32),
        ],
        compiler_params=pltpu.CompilerParams(vmem_limit_bytes=16 * 1024 * 1024),
    )(near, far, columns[:, 2 * depth :])
    partial_value = lax.all_to_all(partial_value, PLANE, 0, 0, tiled=True).astype(jnp.float32)
    steps = jnp.exp2(partial_value[:, row_tiles * half : row_tiles * half + row_tiles] * (1.0 / OCTAVE))
    fixed = partial_value[:, : row_tiles * half].reshape(pieces, row_tiles, half, TILE_SIZE)
    total = jnp.sum(fixed * steps[:, :, None, :], axis=0)
    return total.astype(jnp.bfloat16).transpose(0, 2, 1).reshape(rows, half)


def solution(mesh):
    grid = Mesh(mesh.devices.reshape(-1, 4, 4, 2), ("pair", "y", "x", "core"))
    virt = ("y", "x", "core")
    return jax.shard_map(
        shards,
        mesh=grid,
        in_specs=(P("pair", virt), P("pair", virt), P(virt, "pair"), P(virt, None)),
        out_specs=P("pair", virt),
        check_vma=False,
    )
```
